32 devices in a mesh: dp: 4 (over y, x), expert: 8 (over z, core).
Axes of the slice: x: 2, y: 2, z: 4, core: 2. Of those that a mesh axis runs over, the one named last changes fastest.
Arguments:
- tokens: bfloat16 [2, 4, 1024, 2048], P(None, 'dp', 'expert'), may hold values from -6 to 6
- modality: int32 [2, 4, 1024], P(None, 'dp'), may hold values from 0 to 2, as said below
- norm_gain: float32 [2048], replicated, may hold values from 0.5 to 1.5
- value_proj: bfloat16 [3, 2048, 4096], P(None, 'dp', 'expert'), may hold values from -0.125 to 0.125
- gate_proj: bfloat16 [3, 2048, 4096], P(None, 'dp', 'expert'), may hold values from -0.125 to 0.125
- conv_taps: float32 [4, 4096], P(None, 'expert'), may hold values from -0.5 to 0.5
- conv_bias: float32 [4096], P('expert'), may hold values from -0.5 to 0.5
- state_proj: bfloat16 [3, 4096, 160], P(None, 'expert'), may hold values from -0.09375 to 0.09375
- step_proj: bfloat16 [3, 128, 4096], P(None, None, 'expert'), may hold values from -0.5 to 0.5
- step_bias: float32 [3, 4096], P(None, 'expert'), may hold values from -4.5 to -1.5
- decay_log: float32 [16, 4096], P(None, 'expert'), may hold values from 0 to 2.77
- skip_gain: float32 [4096], P('expert'), may hold values from 0.5 to 1.5
- out_proj: bfloat16 [3, 4096, 2048], P(None, 'expert', 'dp'), may hold values from -0.375 to 0.375
- cotangent: bfloat16 [2, 4, 1024, 2048], P(None, 'dp', 'expert'), may hold values from -6 to 6
Outputs:
- mixed: bfloat16 [2, 4, 1024, 2048], P(None, 'dp', 'expert')
- grad_tokens: bfloat16 [2, 4, 1024, 2048], P(None, 'dp', 'expert')
- grad_norm_gain: float32 [2048], replicated
- grad_value_proj: float32 [3, 2048, 4096], P(None, 'dp', 'expert')
- grad_gate_proj: float32 [3, 2048, 4096], P(None, 'dp', 'expert')
- grad_conv_taps: float32 [4, 4096], P(None, 'expert')
- grad_conv_bias: float32 [4096], P('expert')
- grad_state_proj: float32 [3, 4096, 160], P(None, 'expert')
- grad_step_proj: float32 [3, 128, 4096], P(None, None, 'expert')
- grad_step_bias: float32 [3, 4096], P(None, 'expert')
- grad_decay_log: float32 [16, 4096], P(None, 'expert')
- grad_skip_gain: float32 [4096], P('expert')
- grad_out_proj: float32 [3, 4096, 2048], P(None, 'expert', 'dp')
The draws below stay inside these ranges and needn't reach their ends.
Inputs may be any that keep to these rules, and one draw needn't show every extreme that they name: `modality`: runs of 128 positions in a row share one id; in every sequence the first run is 0 and the last is 2.
All inputs are finite; a program needn't handle non-finite values.
Results may differ from the reference program's by a relative error of at most 0.012.
Values may be sent and summed in bfloat16 or wider, within the bound.
No kernel may reach another device: no remote copies, remote signals or barrier semaphores. Data moves between devices by JAX's collectives and lax.ppermute only.
A program may use at most 448 MiB of HBM per device.

```python
import jax
import jax.numpy as jnp
from jax import lax

D = 2048
INNER = 4096
NSTATE = 16
CONV = 4
RANK = 128
MODES = 3
MICRO = 2
SCAN_BLOCK = 16
SEQS = 4
LENGTH = 1024


def draw_modality(key, part):
    key = jax.random.fold_in(key, 7)
    key_lead, key_other, key_keep = jax.random.split(key, 3)
    span_count = 8
    dominant = jax.random.randint(key_lead, (MICRO, SEQS, 1), 0, 2)
    others = jax.random.randint(key_other, (MICRO, SEQS, span_count), 0, 3)
    keep_mask = jax.random.randint(key_keep, (MICRO, SEQS, span_count), 0, 10) < 7
    span_kinds = jnp.where(keep_mask, dominant, others)
    position = jnp.arange(span_count, dtype=jnp.int32)[None, None, :]
    span_kinds = jnp.where(position == span_count - 1, 2, span_kinds)
    span_kinds = jnp.where(position == 0, 0, span_kinds)
    return jnp.repeat(span_kinds, LENGTH // span_count, axis=2).astype(jnp.int32)


def shard_levels(key, shape, cuts, least, top_value):
    gain = 1.0
    for dim, parts in cuts:
        steps = jax.random.uniform(jax.random.fold_in(jax.random.fold_in(key, 6), dim), (parts,), jnp.float32, least / len(cuts), top_value / len(cuts))
        gain = gain * jnp.repeat(jnp.exp(steps), shape[dim] // parts).reshape((-1,) + (1,) * (len(shape) - 1 - dim))
    return gain


def centred(own_key, shape, spread, bound, cuts=(), held_as=jnp.bfloat16):
    result = jax.random.normal(own_key, shape, jnp.float32) * spread
    if len(cuts) > 0:
        result = shard_levels(own_key, shape, cuts, -0.22, 0.18) * result
    return jnp.clip(result, min=-bound, max=bound).astype(held_as)


def setup_inputs(seed: int = 0) -> dict:
    splits = jax.random.split(jax.random.key(seed), 15)
    tokens = centred(splits[0], (MICRO, SEQS, LENGTH, D), 1.0, 6.0, ((1, 4), (2, 8)))
    modality = draw_modality(jax.random.fold_in(splits[14], 71), 0)
    norm_gain = jnp.clip(1.0 + 0.1 * jax.random.normal(splits[2], (D,), jnp.float32), 0.5, 1.5)
    value_proj = centred(splits[3], (MODES, D, INNER), D ** -0.5, 0.125, ((1, 4), (2, 8)))
    gate_proj = centred(splits[4], (MODES, D, INNER), D ** -0.5, 0.125, ((1, 4), (2, 8)))
    conv_taps = jnp.clip(jax.random.uniform(splits[5], (CONV, INNER), jnp.float32, -0.5, 0.5) * shard_levels(splits[5], (CONV, INNER), ((1, 8),), -0.4, 0.0), -0.5, 0.5)
    conv_bias = jnp.clip(jax.random.uniform(splits[6], (INNER,), jnp.float32, -0.5, 0.5) * shard_levels(splits[6], (INNER,), ((0, 8),), -0.4, 0.0), -0.5, 0.5)
    state_proj = centred(splits[7], (MODES, INNER, RANK + 2 * NSTATE), INNER ** -0.5, 0.09375, ((1, 8),))
    step_proj = centred(splits[8], (MODES, RANK, INNER), RANK ** -0.5, 0.5, ((2, 8),))
    step_bias = jnp.clip(-4.5 + 3.0 * jax.random.uniform(splits[9], (MODES, INNER), jnp.float32) ** shard_levels(splits[9], (MODES, INNER), ((1, 8),), -0.2, 0.2), -4.5, -1.5)
    decay_log = jnp.clip(2.77 * jax.random.uniform(splits[10], (NSTATE, INNER), jnp.float32) ** shard_levels(splits[10], (NSTATE, INNER), ((1, 8),), -0.2, 0.2), 0.0, 2.77)
    skip_gain = jnp.clip(0.5 + 1.0 * jax.random.uniform(splits[11], (INNER,), jnp.float32) ** shard_levels(splits[11], (INNER,), ((0, 8),), -0.2, 0.2), 0.5, 1.5)
    out_proj = centred(splits[12], (MODES, INNER, D), (INNER // 16) ** -0.5, 0.375, ((1, 8), (2, 4)))
    cotangent = centred(splits[13], (MICRO, SEQS, LENGTH, D), 1.0, 6.0, ((1, 4), (2, 8)))
    return dict(tokens=tokens, modality=modality, norm_gain=norm_gain, value_proj=value_proj, gate_proj=gate_proj, conv_taps=conv_taps, conv_bias=conv_bias, state_proj=state_proj, step_proj=step_proj, step_bias=step_bias, decay_log=decay_log, skip_gain=skip_gain, out_proj=out_proj, cotangent=cotangent)


EPSILON = 1e-05
PRECISE = lax.Precision.HIGHEST

@jax.custom_vjp
def low(v):
    return lax.optimization_barrier(v.astype(jnp.bfloat16)).astype(jnp.float32)

@jax.custom_vjp
def low_back(v):
    return v

def low_keep(v):
    return (low(v), None)

def low_pass(kept, grad):
    return (grad,)

def back_keep(v):
    return (v, None)

def back_low(kept, grad):
    return (low(grad),)
low.defvjp(low_keep, low_pass)
low_back.defvjp(back_keep, back_low)

def picked(values, weights, onehot):
    summed = jnp.zeros((values.shape[0], weights.shape[2]), jnp.float32)
    for member in range(MODES):
        summed = summed + onehot[:, member:member + 1] * jnp.dot(values, weights[member], precision=PRECISE)
    return summed

def selective(driven, step_sizes, inject, readout, decay_log, skip_gain):
    decay_rates = -jnp.exp(decay_log)
    block_count = LENGTH // SCAN_BLOCK

    def token_step(hidden_state, pieces):
        driven_now, step_now, inject_now, readout_now = pieces
        hidden_state = jnp.exp(step_now[None, :] * decay_rates) * hidden_state + inject_now[:, None] * (step_now * driven_now)[None, :]
        return (hidden_state, lax.optimization_barrier(jnp.sum(readout_now[:, None] * hidden_state, axis=0)))

    def block_step(hidden_state, pieces):
        return lax.scan(token_step, hidden_state, pieces)
    shaped = tuple((component.reshape((block_count, SCAN_BLOCK) + component.shape[1:]) for component in (driven, step_sizes, inject, readout)))
    _, outputs = lax.scan(jax.checkpoint(block_step), jnp.zeros((NSTATE, INNER), jnp.float32), shaped)
    return outputs.reshape(LENGTH, INNER) + skip_gain * driven

def sequence_forward(params, rows, kinds):
    norm_gain, value_proj, gate_proj, conv_taps, conv_bias, state_proj, step_proj, step_bias, decay_log, skip_gain, out_proj = params
    onehot = (kinds[:, None] == jnp.arange(MODES, dtype=jnp.int32)[None, :]).astype(jnp.float32)
    scales = lax.rsqrt(lax.optimization_barrier(jnp.mean(rows * rows, axis=1, keepdims=True)) + EPSILON)
    normed = low(rows * scales * norm_gain)
    values_pre = low_back(picked(normed, value_proj, onehot))
    gate_pre = low_back(picked(normed, gate_proj, onehot))
    padded = jnp.concatenate([jnp.zeros((CONV - 1, INNER), jnp.float32), values_pre], axis=0)
    convolved = conv_bias + conv_taps[0] * padded[:LENGTH]
    for offset in range(1, CONV):
        convolved = convolved + conv_taps[offset] * padded[offset:offset + LENGTH]
    driven = jax.nn.silu(convolved)
    projected = low_back(picked(low(driven), state_proj, onehot))
    step_low = low(projected[:, :RANK])
    inject = projected[:, RANK:RANK + NSTATE]
    readout = projected[:, RANK + NSTATE:]
    step_pre = low_back(picked(step_low, step_proj, onehot) + jnp.dot(onehot, step_bias, precision=PRECISE))
    step_sizes = jax.nn.softplus(step_pre)
    mixed_inner = selective(driven, step_sizes, inject, readout, decay_log, skip_gain) * jax.nn.silu(gate_pre)
    return rows + picked(low(mixed_inner), out_proj, onehot)

def reference(tokens, modality, norm_gain, value_proj, gate_proj, conv_taps, conv_bias, state_proj, step_proj, step_bias, decay_log, skip_gain, out_proj, cotangent):
    params = tuple((weight.astype(jnp.float32) for weight in (norm_gain, value_proj, gate_proj, conv_taps, conv_bias, state_proj, step_proj, step_bias, decay_log, skip_gain, out_proj)))
    rows_all = tokens.astype(jnp.float32).reshape(MICRO * SEQS, LENGTH, D)
    kinds_all = modality.reshape(MICRO * SEQS, LENGTH)

    def forward(params, rows_all):

        def one_sequence(unused, pieces):
            return (unused, jax.checkpoint(sequence_forward)(params, pieces[0], pieces[1]))
        _, outputs = lax.scan(one_sequence, jnp.zeros((), jnp.float32), (rows_all, kinds_all))
        return outputs
    mixed, pullback = jax.vjp(forward, params, rows_all)
    grads, grad_rows = pullback(cotangent.astype(jnp.float32).reshape(MICRO * SEQS, LENGTH, D))
    shape_out = (MICRO, SEQS, LENGTH, D)
    return (mixed.reshape(shape_out).astype(jnp.bfloat16), grad_rows.reshape(shape_out).astype(jnp.bfloat16), grads[0], grads[1], grads[2], grads[3], grads[4], grads[5], grads[6], grads[7], grads[8], grads[9], grads[10])
```

```python
import functools
import math

import jax
import jax.numpy as jnp
from jax import lax
from jax.experimental import pallas as pl
from jax.experimental.pallas import tpu as pltpu
from jax.sharding import PartitionSpec as P

MODES = 3
EPSILON = 1e-05
ROWS = 128
GROUP = 8
LANES = 128
LOG2E = math.log2(math.e)
LN2 = math.log(2.0)
F32 = jnp.float32
BF16 = jnp.bfloat16


def dot(left, right, left_dim, right_dim):
    return lax.dot_general(
        left, right, (((left_dim,), (right_dim,)), ((), ())), preferred_element_type=F32
    )


def softplus(v):
    return jnp.maximum(v, 0.0) + jnp.log1p(jnp.exp(-jnp.abs(v)))


def whole(array):
    rank = len(array.shape)
    return pl.BlockSpec(array.shape, lambda *_: (0,) * rank)


def run(body, grid, scalars, ins, outs, scratch, flops, name, after=(), aliases={}, share=0.25):
    in_arrays = [array for array, _ in ins]
    out_shapes = [shape for shape, _ in outs]
    moved = sum(math.prod(a.shape) * a.dtype.itemsize for a in in_arrays + out_shapes)
    kept = len(scalars) + len(ins)

    def without(*refs):
        body(*refs[:kept], *refs[kept + len(after) :])

    return pl.pallas_call(
        without,
        grid_spec=pltpu.PrefetchScalarGridSpec(
            num_scalar_prefetch=len(scalars),
            grid=grid,
            in_specs=[spec for _, spec in ins] + [pl.BlockSpec(memory_space=pl.ANY)] * len(after),
            out_specs=[spec for _, spec in outs],
            scratch_shapes=scratch,
        ),
        out_shape=out_shapes,
        compiler_params=pltpu.CompilerParams(
            dimension_semantics=("arbitrary",) * len(grid), vmem_limit_bytes=60 * 1024 * 1024
        ),
        cost_estimate=pl.CostEstimate(
            flops=int(flops * share), bytes_accessed=int(moved * share), transcendentals=0
        ),
        input_output_aliases=aliases,
        name=name,
    )(*scalars, *in_arrays, *after)


def shaped(shape, dtype):
    return jax.ShapeDtypeStruct(shape, dtype)


def by_pair(kinds, step, work):
    first, second = kinds[2 * step], kinds[2 * step + 1]

    @pl.when(first == second)
    def _():
        work(first, slice(0, 2 * ROWS))

    @pl.when(first != second)
    def _():
        work(first, slice(0, ROWS))
        work(second, slice(ROWS, 2 * ROWS))


def into_channels(x, rows, kind, weights, offs, weight_dim):
    total = None
    for piece, weight in enumerate(weights):
        width = weight.shape[weight_dim + 1]
        columns = pl.ds(pl.multiple_of(offs[piece], width), width)
        part = dot(x[rows, columns], weight[kind], 1, weight_dim)
        total = part if total is None else total + part
    return total


def pair_spec(width):
    return pl.BlockSpec((2 * ROWS, width), lambda i, *_: (i, 0))


def value_kernel(pieces, kinds, offs, x, *refs):
    weights = refs[:pieces]
    taps, bias, state_t, pre_out, conv_out, part_out, ext, driven = refs[pieces:]
    step = pl.program_id(0)
    size = 2 * ROWS

    @pl.when(step == 0)
    def _():
        ext[0:GROUP, :] = jnp.zeros((GROUP, ext.shape[1]), F32)

    @pl.when(step > 0)
    def _():
        ext[0:GROUP, :] = ext[size : size + GROUP, :]

    def project(kind, rows):
        pre_out[rows, :] = into_channels(x, rows, kind, weights, offs, 0)

    by_pair(kinds, step, project)
    total = pre_out[...]
    ext[GROUP : GROUP + size, :] = total
    convolved = bias[...] + taps[3:4, :] * total
    for tap in range(3):
        start = GROUP - 3 + tap
        convolved = convolved + taps[tap : tap + 1, :] * ext[start : start + size, :]
    conv_out[...] = convolved
    driven[...] = (convolved * jax.nn.sigmoid(convolved)).astype(BF16)

    def narrow(kind, rows):
        part_out[:, rows] = dot(state_t[kind], driven[rows, :], 1, 1)

    by_pair(kinds, step, narrow)


def value_call(kinds, offs, x, weights, taps, bias, state_t, after=()):
    length, width = x.shape
    channels = taps.shape[1]
    wide = state_t.shape[1]
    return run(
        functools.partial(value_kernel, len(weights)),
        (length // (2 * ROWS),),
        (kinds, offs),
        [(x, pair_spec(width))]
        + [(w, whole(w)) for w in weights]
        + [(taps, whole(taps)), (bias, whole(bias)), (state_t, whole(state_t))],
        [
            (shaped((length, channels), F32), pair_spec(channels)),
            (shaped((length, channels), F32), pair_spec(channels)),
            (shaped((wide, length), F32), pl.BlockSpec((wide, 2 * ROWS), lambda i, *_: (0, i))),
        ],
        [pltpu.VMEM((2 * ROWS + GROUP, channels), F32), pltpu.VMEM((2 * ROWS, channels), BF16)],
        2 * length * width * channels,
        "value_in",
        after=after,
    )


def gate_kernel(pieces, kinds, offs, x, *refs):
    weights, out = refs[:pieces], refs[pieces]

    def project(kind, rows):
        out[rows, :] = into_channels(x, rows, kind, weights, offs, 0)

    by_pair(kinds, pl.program_id(0), project)


def gate_call(kinds, offs, x, weights, after=()):
    length, width = x.shape
    channels = weights[0].shape[2]
    return run(
        functools.partial(gate_kernel, len(weights)),
        (length // (2 * ROWS),),
        (kinds, offs),
        [(x, pair_spec(width))] + [(w, whole(w)) for w in weights],
        [(shaped((length, channels), F32), pair_spec(channels))],
        [],
        2 * length * width * channels,
        "gate_in",
        after=after,
        share=4,
    )[0]


def back_out_kernel(pieces, kinds, offs, upstream, gate, scanned, *refs):
    weights = refs[:pieces]
    back_out, gate_back_out = refs[pieces:]

    def project(kind, rows):
        back_out[rows, :] = into_channels(upstream, rows, kind, weights, offs, 1)

    by_pair(kinds, pl.program_id(0), project)
    total = back_out[...]
    pre = gate[...]
    sig = jax.nn.sigmoid(pre)
    back_out[...] = total * (pre * sig)
    slope = sig * (1.0 + pre * (1.0 - sig))
    gate_back_out[...] = (total * scanned[...] * slope).astype(BF16)


def back_out_call(kinds, offs, upstream, gate, scanned, weights, after=()):
    length, width = upstream.shape
    channels = gate.shape[1]
    return run(
        functools.partial(back_out_kernel, len(weights)),
        (length // (2 * ROWS),),
        (kinds, offs),
        [
            (upstream, pair_spec(width)),
            (gate, pair_spec(channels)),
            (scanned, pair_spec(channels)),
        ]
        + [(w, whole(w)) for w in weights],
        [
            (shaped((length, channels), F32), pair_spec(channels)),
            (shaped((length, channels), BF16), pair_spec(channels)),
        ],
        [],
        2 * length * width * channels,
        "back_out",
        after=after,
    )


def out_kernel(pieces, kinds, offs, mixed, *refs):
    weights, out = refs[:pieces], refs[pieces]

    def project(kind, rows):
        for piece, weight in enumerate(weights):
            width = weight.shape[2]
            columns = pl.ds(pl.multiple_of(offs[piece], width), width)
            out[rows, columns] = dot(mixed[rows, :], weight[kind], 1, 0).astype(BF16)

    by_pair(kinds, pl.program_id(0), project)


def out_call(kinds, offs, mixed, weights, after=()):
    length, channels = mixed.shape
    width = weights[0].shape[2] * len(weights)
    return run(
        functools.partial(out_kernel, len(weights)),
        (length // (2 * ROWS),),
        (kinds, offs),
        [(mixed, pair_spec(channels))] + [(w, whole(w)) for w in weights],
        [(shaped((length, width), BF16), pair_spec(width))],
        [],
        2 * length * width * channels,
        "out",
        after=after,
    )[0]


def normed_back_kernel(pieces, kinds, offs, value_back, gate_back, x, *refs):
    values, gates = refs[:pieces], refs[pieces : 2 * pieces]
    out, gain_out = refs[2 * pieces :]
    step = pl.program_id(0)

    @pl.when(step == 0)
    def _():
        gain_out[...] = jnp.zeros(gain_out.shape, F32)

    def project(kind, rows):
        for piece in range(pieces):
            width = values[piece].shape[1]
            columns = pl.ds(pl.multiple_of(offs[piece], width), width)
            total = dot(value_back[rows, :], values[piece][kind], 1, 1)
            total = total + dot(gate_back[rows, :], gates[piece][kind], 1, 1)
            out[rows, columns] = total.astype(BF16)
            product = total * x[rows, columns].astype(F32)
            gain_out[:, columns] += jnp.sum(product, axis=0, keepdims=True)

    by_pair(kinds, step, project)


def normed_back_call(kinds, offs, value_back, gate_back, x, values, gates, after=()):
    length, channels = value_back.shape
    width = values[0].shape[1] * len(values)
    return run(
        functools.partial(normed_back_kernel, len(values)),
        (length // (2 * ROWS),),
        (kinds, offs),
        [
            (value_back, pair_spec(channels)),
            (gate_back, pair_spec(channels)),
            (x, pair_spec(width)),
        ]
        + [(w, whole(w)) for w in values + gates],
        [
            (shaped((length, width), BF16), pair_spec(width)),
            (shaped((1, width), F32), pl.BlockSpec((1, width), lambda *_: (0, 0))),
        ],
        [],
        4 * length * width * channels,
        "normed_back",
        after=after,
    )


def sort_kinds(kinds):
    count = kinds.shape[0]
    index = jnp.arange(count, dtype=jnp.int32)
    ahead = (kinds[None, :] < kinds[:, None]) | (
        (kinds[None, :] == kinds[:, None]) & (index[None, :] < index[:, None])
    )
    rank = jnp.sum(ahead.astype(jnp.int32), axis=1)
    here = rank[None, :] == index[:, None]
    pick = lambda numbers: jnp.sum(jnp.where(here, numbers[None, :], 0), axis=1).astype(jnp.int32)
    return pick(index), pick(kinds)


def weight_kernel(micros, pieces, halves, wide_left, count, order, kinds, offs, *refs):
    wides, narrows = refs[: 2 * micros], refs[2 * micros : 4 * micros]
    ends = 4 * micros + pieces * halves
    outs, acc = refs[4 * micros : ends], refs[ends:-2]
    wide, narrow = refs[-2:]
    step = pl.program_id(0)

    @pl.when(step == 0)
    def _():
        for piece in range(pieces):
            acc[piece][...] = jnp.zeros(acc[piece].shape, F32)

    for side in range(2):
        rows = slice(side * ROWS, (side + 1) * ROWS)
        for micro in range(micros):

            @pl.when(order[2 * step + side] // count == micro)
            def _(side=side, rows=rows, micro=micro):
                wide[rows, :] = wides[2 * micro + side][...]
                narrow[rows, :] = narrows[2 * micro + side][...]

    def add(kind, rows):
        for piece in range(pieces):
            width = acc[piece].shape[1 if wide_left else 2]
            columns = pl.ds(pl.multiple_of(offs[piece], width), width)
            left, right = wide[rows, columns], narrow[rows, :]
            acc[piece][kind] += dot(left, right, 0, 0) if wide_left else dot(right, left, 0, 0)

    by_pair(kinds, step, add)

    @pl.when(step == pl.num_programs(0) - 1)
    def _():
        for piece in range(pieces):
            height = acc[piece].shape[1] // halves
            for half in range(halves):
                rows = slice(half * height, (half + 1) * height)
                outs[piece * halves + half][...] = acc[piece][:, rows, :].astype(BF16)


def weight_call(sorted_kinds, offs, wides, narrows, pieces, wide_left, name, halves=1, after=()):
    order, kinds = sorted_kinds
    micros = len(wides)
    length, width = wides[0].shape
    channels = narrows[0].shape[1]
    count = length // ROWS
    part = width // pieces
    shape = (MODES, part, channels) if wide_left else (MODES, channels, part)
    cut = (MODES, shape[1] // halves, shape[2])

    def specs(columns):
        return [
            pl.BlockSpec((ROWS, columns), lambda i, order, *_: (order[2 * i] % count, 0)),
            pl.BlockSpec((ROWS, columns), lambda i, order, *_: (order[2 * i + 1] % count, 0)),
        ]

    return run(
        functools.partial(weight_kernel, micros, pieces, halves, wide_left, count),
        (micros * count // 2,),
        (order, kinds, offs),
        [(w, spec) for w in wides for spec in specs(width)]
        + [(n, spec) for n in narrows for spec in specs(channels)],
        [(shaped(cut, BF16), pl.BlockSpec(cut, lambda *_: (0, 0, 0)))] * (pieces * halves),
        [pltpu.VMEM(shape, F32)] * pieces
        + [pltpu.VMEM((2 * ROWS, width), BF16), pltpu.VMEM((2 * ROWS, channels), BF16)],
        2 * micros * length * width * channels,
        name,
        after=after,
    )


def fold_rows(parts):
    row = lax.broadcasted_iota(jnp.int32, (GROUP, LANES), 0)
    low4 = row < 4
    stage = []
    for u in range(4):
        first, second = parts[u], parts[u + 4]
        kept = jnp.where(low4, first, second)
        other = jnp.where(low4, second, first)
        stage.append(kept + pltpu.roll(other, 4, 0))
    low2 = (row & 3) < 2
    halves = []
    for u in range(2):
        first = stage[u] + pltpu.roll(stage[u], GROUP - 2, 0)
        second = stage[u + 2] + pltpu.roll(stage[u + 2], 2, 0)
        halves.append(jnp.where(low2, first, second))
    low1 = (row & 1) < 1
    first = halves[0] + pltpu.roll(halves[0], GROUP - 1, 0)
    second = halves[1] + pltpu.roll(halves[1], 1, 0)
    return jnp.where(low1, first, second)


HALVES = (slice(0, GROUP), slice(GROUP, 2 * GROUP))
UNROLL = 16
UNROLL_BACK = 16
FOLD = 4


def lanes_of(tile):
    return slice(tile * LANES, (tile + 1) * LANES)


def spread(source, target):
    for t in range(ROWS):
        target[t] = jnp.broadcast_to(source[:, t : t + 1], target.shape[1:])


def by_tile(value, target):
    for c in range(target.shape[0]):
        target[c] = value[:, lanes_of(c)]


def everywhere(ref, tile, row):
    return ref[tile, pl.ds(row, GROUP, stride=0), :]


def fold_all(parts, target):
    def some(index, _):
        for step in range(FOLD):
            base = pl.multiple_of((index * FOLD + step) * GROUP, GROUP)
            for c in range(target.shape[1] // LANES):
                rows = [parts[base + u, :, lanes_of(c)] for u in range(GROUP)]
                target[pl.ds(base, GROUP), lanes_of(c)] = fold_rows(rows)
        return 0

    lax.fori_loop(0, ROWS // (GROUP * FOLD), some, 0)


def spread_rows(value, target):
    for t in range(ROWS):
        target[t] = jnp.broadcast_to(value[t : t + 1, :], target.shape[1:])


def rates_of(decay, tiles):
    return [[-LOG2E * jnp.exp(decay[half, lanes_of(c)]) for half in HALVES] for c in range(tiles)]


def scan_kernel(
    kinds,
    proj,
    step_w,
    step_b,
    conv,
    gate,
    decay,
    skip,
    states_out,
    scanned_out,
    pre_out,
    mixed_out,
    held,
    steps,
    drives,
    sums,
    injects,
    readouts,
    parts,
):
    block = pl.program_id(0)
    kind = kinds[block]
    rank = step_w.shape[1]
    width, channels = decay.shape
    tiles = channels // LANES

    @pl.when(block == 0)
    def _():
        held[...] = jnp.zeros(held.shape, F32)

    low = proj[0:rank, :].astype(BF16)
    pre = dot(low, step_w[kind], 0, 0) + step_b[pl.ds(kind, 1), :]
    pre_out[...] = pre
    size = softplus(pre)
    convolved = conv[...]
    driven = convolved * jax.nn.sigmoid(convolved)
    spread_rows(size, steps)
    spread_rows(size * driven, drives)
    spread(proj[rank : rank + width, :], injects)
    spread(proj[rank + width : rank + 2 * width, :], readouts)
    rates = rates_of(decay, tiles)

    def some(index, states):
        states = [list(tile) for tile in states]
        base = index * UNROLL
        for u in range(UNROLL):
            row = base + u
            into = [injects[row, half, :] for half in HALVES]
            out = [readouts[row, half, :] for half in HALVES]
            for c in range(tiles):
                size_now = steps[row, :, lanes_of(c)]
                drive_now = drives[row, :, lanes_of(c)]
                read = None
                for h, half in enumerate(HALVES):
                    state = jnp.exp2(size_now * rates[c][h]) * states[c][h] + into[h] * drive_now
                    states[c][h] = state
                    states_out[row, half, lanes_of(c)] = state
                    read = out[h] * state if read is None else read + out[h] * state
                parts[row, :, lanes_of(c)] = read
        return tuple(tuple(tile) for tile in states)

    start = tuple(tuple(held[half, lanes_of(c)] for half in HALVES) for c in range(tiles))
    final = lax.fori_loop(0, ROWS // UNROLL, some, start)
    for c in range(tiles):
        for h, half in enumerate(HALVES):
            held[half, lanes_of(c)] = final[c][h]
    fold_all(parts, sums)
    scanned = sums[...] + skip[...] * driven
    scanned_out[...] = scanned
    gated = gate[...]
    mixed_out[...] = (scanned * (gated * jax.nn.sigmoid(gated))).astype(BF16)


def scan_call(kinds, proj, step_w, step_b, conv, gate, decay, skip, after=()):
    length, channels = conv.shape
    width = decay.shape[0]
    wide = proj.shape[0]
    block = lambda i, *_: (i, 0)
    narrow = pl.BlockSpec((ROWS, channels), block)
    return run(
        scan_kernel,
        (length // ROWS,),
        (kinds,),
        [
            (proj, pl.BlockSpec((wide, ROWS), lambda i, *_: (0, i))),
            (step_w, whole(step_w)),
            (step_b, whole(step_b)),
            (conv, narrow),
            (gate, narrow),
            (decay, whole(decay)),
            (skip, whole(skip)),
        ],
        [
            (
                shaped((length, width, channels), F32),
                pl.BlockSpec((ROWS, width, channels), lambda i, *_: (i, 0, 0)),
            ),
            (shaped((length, channels), F32), narrow),
            (shaped((length, channels), F32), narrow),
            (shaped((length, channels), BF16), narrow),
        ],
        [
            pltpu.VMEM((width, channels), F32),
            pltpu.VMEM((ROWS, GROUP, channels), F32),
            pltpu.VMEM((ROWS, GROUP, channels), F32),
            pltpu.VMEM((ROWS, channels), F32),
            pltpu.VMEM((ROWS, width, LANES), F32),
            pltpu.VMEM((ROWS, width, LANES), F32),
            pltpu.VMEM((ROWS, GROUP, channels), F32),
        ],
        length * width * channels * 3200,
        "scan",
        after=after,
        share=1,
    )


def scan_back_kernel(
    first,
    kinds,
    proj,
    step_w,
    conv,
    pre_in,
    back,
    states,
    before,
    decay,
    skip,
    *rest,
):
    (
        later_part,
        later_driven,
        later_queue,
        part_out,
        driven_out,
        queue_out,
        decay_out,
        skip_out,
        bias_out,
        step_w_out,
        queue,
        rate_sum,
        steps,
        drives,
        backs,
        drive_sums,
        rate_sums,
        injects,
        readouts,
        drive_parts,
        rate_parts,
        inject_parts,
        read_parts,
    ) = rest
    blocks = pl.num_programs(0)
    turn = pl.program_id(0)
    kind = kinds[first + blocks - 1 - turn]
    rank = step_w.shape[1]
    width, channels = decay.shape
    tiles = channels // LANES

    @pl.when(turn == 0)
    def _():
        queue[...] = later_queue[...]
        rate_sum[...] = jnp.zeros(rate_sum.shape, F32)
        skip_out[...] = jnp.zeros(skip_out.shape, F32)
        bias_out[...] = jnp.zeros(bias_out.shape, F32)
        step_w_out[...] = jnp.zeros(step_w_out.shape, F32)

    pre = pre_in[...]
    size = softplus(pre)
    convolved = conv[...]
    driven = convolved * jax.nn.sigmoid(convolved)
    by_tile(size, steps)
    by_tile(size * driven, drives)
    by_tile(back[...], backs)
    spread(proj[rank : rank + width, :], injects)
    spread(proj[rank + width : rank + 2 * width, :], readouts)
    rates = rates_of(decay, tiles)
    first_block = first + blocks - 1 - turn == 0

    def some(turned, carried):
        adjoints, totals = carried
        adjoints, totals = [list(tile) for tile in adjoints], [list(tile) for tile in totals]
        index = ROWS // UNROLL_BACK - 1 - turned
        base = index * UNROLL_BACK
        last = base + UNROLL_BACK - 1
        groups = [
            [ref[c, pl.ds(pl.multiple_of(base, GROUP), UNROLL_BACK), :] for c in range(tiles)]
            for ref in (steps, drives, backs)
        ]
        now = [[states[last, half, lanes_of(c)] for half in HALVES] for c in range(tiles)]
        for u in reversed(range(UNROLL_BACK)):
            row = base + u
            into = [injects[row, half, :] for half in HALVES]
            out = [readouts[row, half, :] for half in HALVES]
            inject_sum, read_sum = [None, None], [None, None]
            for c in range(tiles):
                size_now = jnp.broadcast_to(groups[0][c][u : u + 1], (GROUP, LANES))
                drive_now = jnp.broadcast_to(groups[1][c][u : u + 1], (GROUP, LANES))
                back_now = jnp.broadcast_to(groups[2][c][u : u + 1], (GROUP, LANES))
                drive_part, rate_part = None, None
                for h, half in enumerate(HALVES):
                    if u > 0:
                        earlier = states[row - 1, half, lanes_of(c)]
                    else:
                        inside = states[jnp.maximum(base - 1, 0), half, lanes_of(c)]
                        edge = jnp.where(first_block, 0.0, before[0, half, lanes_of(c)])
                        earlier = jnp.where(index == 0, edge, inside)
                    state = now[c][h]
                    now[c][h] = earlier
                    adjoint = out[h] * back_now + adjoints[c][h]
                    term = adjoint * into[h]
                    drive_part = term if h == 0 else drive_part + term
                    term = adjoint * drive_now
                    inject_sum[h] = term if c == 0 else inject_sum[h] + term
                    term = state * back_now
                    read_sum[h] = term if c == 0 else read_sum[h] + term
                    adjoint = jnp.exp2(size_now * rates[c][h]) * adjoint
                    adjoints[c][h] = adjoint
                    flow = adjoint * earlier
                    term = rates[c][h] * flow
                    rate_part = term if h == 0 else rate_part + term
                    totals[c][h] = totals[c][h] + size_now * flow
                drive_parts[row, :, lanes_of(c)] = drive_part
                rate_parts[row, :, lanes_of(c)] = rate_part
            for h, half in enumerate(HALVES):
                inject_parts[row, half, :] = inject_sum[h]
                read_parts[row, half, :] = read_sum[h]
        return tuple(tuple(tile) for tile in adjoints), tuple(tuple(tile) for tile in totals)

    tile = lambda ref: tuple(
        tuple(ref[half, lanes_of(c)] for half in HALVES) for c in range(tiles)
    )
    adjoints, totals = lax.fori_loop(0, ROWS // UNROLL_BACK, some, (tile(queue), tile(rate_sum)))
    for c in range(tiles):
        for h, half in enumerate(HALVES):
            queue[half, lanes_of(c)] = adjoints[c][h]
            rate_sum[half, lanes_of(c)] = totals[c][h]

    @pl.when(turn == blocks - 1)
    def _():
        decay_out[...] = -jnp.exp(decay[...]) * rate_sum[...]
        queue_out[...] = queue[...]

    fold_all(drive_parts, drive_sums)
    fold_all(rate_parts, rate_sums)
    lane = lax.broadcasted_iota(jnp.int32, (width, LANES), 1)
    inject_back = jnp.zeros((width, LANES), F32)
    read_back = jnp.zeros((width, LANES), F32)
    for t in range(ROWS):
        inject_now = jnp.sum(inject_parts[t], axis=1, keepdims=True)
        inject_back = jnp.where(lane == t, inject_now, inject_back)
        read_now = jnp.sum(read_parts[t], axis=1, keepdims=True)
        read_back = jnp.where(lane == t, read_now, read_back)

    grad_scanned = back[...]
    summed = drive_sums[...]
    driven_out[...] = size * summed + skip[...] * grad_scanned
    step_grad = driven * summed + LN2 * rate_sums[...]
    step_back = (step_grad * jax.nn.sigmoid(pre)).astype(BF16)
    skip_out[...] += jnp.sum(grad_scanned * driven, axis=0, keepdims=True)
    bias_out[pl.ds(kind, 1), :] += jnp.sum(step_back.astype(F32), axis=0, keepdims=True)
    low = proj[0:rank, :].astype(BF16)
    step_w_out[kind] += dot(low, step_back, 1, 0)
    part_out[0:rank, :] = dot(step_w[kind], step_back, 1, 1)
    part_out[rank : rank + width, :] = inject_back
    part_out[rank + width : rank + 2 * width, :] = read_back


def scan_back_call(
    kinds, proj, step_w, conv, pre, back, states, decay, skip, first, count, later, after=()
):
    length, channels = conv.shape
    width = decay.shape[0]
    wide = proj.shape[0]
    at = lambda i: first + count - 1 - i
    narrow = pl.BlockSpec((ROWS, channels), lambda i, *_: (at(i), 0))
    turned = pl.BlockSpec((wide, ROWS), lambda i, *_: (0, at(i)))
    fixed = lambda *_: (0, 0)
    step_shape = (MODES, step_w.shape[1], channels)
    row = shaped((1, channels), F32)
    state = shaped((width, channels), F32)
    unread = pl.BlockSpec(memory_space=pl.ANY)
    ins = [
        (proj, turned),
        (step_w, whole(step_w)),
        (conv, narrow),
        (pre, narrow),
        (back, narrow),
        (states, pl.BlockSpec((ROWS, width, channels), lambda i, *_: (at(i), 0, 0))),
        (
            states,
            pl.BlockSpec(
                (1, width, channels), lambda i, *_: (jnp.maximum(at(i) * ROWS - 1, 0), 0, 0)
            ),
        ),
        (decay, whole(decay)),
        (skip, whole(skip)),
    ]
    if later is None:
        later = jnp.zeros((8, LANES), F32), jnp.zeros((8, LANES), F32), jnp.zeros(state.shape, F32)
        aliases = {}
    else:
        aliases = {len(ins) + 1: 0, len(ins) + 2: 1}
    ins += [(later[0], unread), (later[1], unread), (later[2], whole(later[2]))]
    return run(
        functools.partial(scan_back_kernel, first),
        (count,),
        (kinds,),
        ins,
        [
            (shaped((wide, length), F32), turned),
            (shaped((length, channels), F32), narrow),
            (state, pl.BlockSpec(state.shape, fixed)),
            (state, pl.BlockSpec(state.shape, fixed)),
            (row, pl.BlockSpec(row.shape, fixed)),
            (shaped((MODES, channels), F32), pl.BlockSpec((MODES, channels), fixed)),
            (shaped(step_shape, F32), pl.BlockSpec(step_shape, lambda *_: (0, 0, 0))),
        ],
        [
            pltpu.VMEM((width, channels), F32),
            pltpu.VMEM((width, channels), F32),
            pltpu.VMEM((channels // LANES, ROWS, LANES), F32),
            pltpu.VMEM((channels // LANES, ROWS, LANES), F32),
            pltpu.VMEM((channels // LANES, ROWS, LANES), F32),
            pltpu.VMEM((ROWS, channels), F32),
            pltpu.VMEM((ROWS, channels), F32),
            pltpu.VMEM((ROWS, width, LANES), F32),
            pltpu.VMEM((ROWS, width, LANES), F32),
            pltpu.VMEM((ROWS, GROUP, channels), F32),
            pltpu.VMEM((ROWS, GROUP, channels), F32),
            pltpu.VMEM((ROWS, width, LANES), F32),
            pltpu.VMEM((ROWS, width, LANES), F32),
        ],
        count * ROWS * width * channels * 5600,
        "scan_back",
        after=after,
        aliases=aliases,
        share=1,
    )


def driven_back_kernel(
    kinds, part, state_t, driven_in, conv, pre, taps, value_out, taps_out, bias_out, state_out, ext
):
    blocks = pl.num_programs(0)
    turn = pl.program_id(0)
    kind = kinds[blocks - 1 - turn]

    @pl.when(turn == 0)
    def _():
        ext[ROWS : ROWS + GROUP, :] = jnp.zeros((GROUP, ext.shape[1]), F32)
        taps_out[...] = jnp.zeros(taps_out.shape, F32)
        bias_out[...] = jnp.zeros(bias_out.shape, F32)
        state_out[...] = jnp.zeros(state_out.shape, F32)

    @pl.when(turn > 0)
    def _():
        ext[ROWS : ROWS + GROUP, :] = ext[0:GROUP, :]

    low = part[...].astype(BF16)
    convolved = conv[...]
    sig = jax.nn.sigmoid(convolved)
    driven = (convolved * sig).astype(BF16)
    state_out[kind] += dot(low, driven, 1, 0)
    grad_driven = driven_in[...] + dot(low, state_t[kind], 0, 0)
    grad = grad_driven * (sig * (1.0 + convolved * (1.0 - sig)))
    ext[0:ROWS, :] = grad
    bias_out[...] += jnp.sum(grad, axis=0, keepdims=True)
    values = pre[...]
    total = taps[3:4, :] * grad
    taps_out[3:4, :] += jnp.sum(grad * values, axis=0, keepdims=True)
    for tap in range(3):
        later = ext[3 - tap : 3 - tap + ROWS, :]
        total = total + taps[tap : tap + 1, :] * later
        taps_out[tap : tap + 1, :] += jnp.sum(later * values, axis=0, keepdims=True)
    value_out[...] = total.astype(BF16)


def driven_back_call(kinds, part, state_t, driven, conv, pre, taps, after=()):
    length, channels = conv.shape
    wide = part.shape[0]
    count = length // ROWS
    narrow = pl.BlockSpec((ROWS, channels), lambda i, *_: (count - 1 - i, 0))
    fixed = lambda *_: (0, 0)
    state_shape = (MODES, wide, channels)
    return run(
        driven_back_kernel,
        (count,),
        (kinds,),
        [
            (part, pl.BlockSpec((wide, ROWS), lambda i, *_: (0, count - 1 - i))),
            (state_t, whole(state_t)),
            (driven, narrow),
            (conv, narrow),
            (pre, narrow),
            (taps, whole(taps)),
        ],
        [
            (shaped((length, channels), BF16), narrow),
            (shaped(taps.shape, F32), pl.BlockSpec(taps.shape, fixed)),
            (shaped((1, channels), F32), pl.BlockSpec((1, channels), fixed)),
            (shaped(state_shape, F32), pl.BlockSpec(state_shape, lambda *_: (0, 0, 0))),
        ],
        [pltpu.VMEM((ROWS + GROUP, channels), F32)],
        4 * length * wide * channels,
        "driven_back",
        after=after,
        share=4,
    )


def swap(array, flip):
    return lax.ppermute(array, "dp", [(source, source ^ flip) for source in range(4)])


def cross(array, flip):
    return lax.ppermute(array, "expert", [(source, source ^ flip) for source in range(8)])


def then(array, *earlier):
    return lax.optimization_barrier((array, *earlier))[0]


def first_hop(shard, dim, square, *earlier):
    sent = then(shard, *earlier)
    if not square:
        return [lax.all_gather(sent, "dp", axis=dim, tiled=True)]
    return [swap(sent, 1), swap(sent, 2)]


def second_hop(shard, near, *earlier):
    if len(near) == 1:
        return near
    by_x, by_y = near
    half = shard.shape[1] // 2
    first = swap(then(by_x[:, :half], *earlier), 2)
    second = swap(then(by_y[:, half:], *earlier), 1)
    return [shard, by_x, by_y, jnp.concatenate([first, second], axis=1)]


def send_pieces(pieces, dim):
    if len(pieces) == 1:
        return [lax.psum_scatter(pieces[0], "dp", scatter_dimension=dim, tiled=True)]
    return [swap(piece, flip) for flip, piece in enumerate(pieces) if flip > 0]


def sum_pieces(pieces, received):
    total = received[0].astype(F32)
    for piece in received[1:]:
        total = total + piece.astype(F32)
    return total if len(pieces) == 1 else total + pieces[0].astype(F32)


def scatter_halves(pieces):
    own, to_x, to_y, to_both = [pieces[2 * piece : 2 * piece + 2] for piece in range(4)]
    joined = lambda piece, more: (piece.astype(F32) + more.astype(F32)).astype(BF16)
    along_y = joined(to_y[0], swap(to_both[0], 1))
    along_x = joined(to_x[1], swap(to_both[1], 2))
    first = own[0].astype(F32) + swap(to_x[0], 1).astype(F32) + swap(along_y, 2).astype(F32)
    second = own[1].astype(F32) + swap(to_y[1], 2).astype(F32) + swap(along_x, 1).astype(F32)
    return jnp.concatenate([first, second], axis=1)


def sum_dp(array, square):
    sent = array.astype(BF16)
    if not square:
        return lax.psum(sent, "dp").astype(F32)
    total = sent.astype(F32)
    for flip in (1, 2, 3):
        total = total + swap(sent, flip).astype(F32)
    return total


def sum_cores(part, square):
    if not square:
        return lax.psum(part, "expert")
    half = part.shape[0] // 2
    lower = (lax.axis_index("expert") & 1) == 0
    top, bottom = part[:half], part[half:]
    return jnp.where(lower, top, bottom) + cross(jnp.where(lower, bottom, top), 1)


def sum_chips(pair, square, *earlier):
    if not square:
        return pair
    sent = then(pair.astype(BF16), *earlier)
    total = sent.astype(F32)
    for flip in (2, 4, 6):
        total = total + cross(sent, flip).astype(F32)
    return total


def join_cores(total, square, kept_as):
    total = total.astype(kept_as)
    if not square:
        return total
    other = cross(total, 1)
    lower = (lax.axis_index("expert") & 1) == 0
    return jnp.concatenate(
        [jnp.where(lower, total, other), jnp.where(lower, other, total)], axis=0
    )


def sum_row_dp(row, square):
    if not square:
        return lax.psum(row, "dp")
    return row + swap(row, 1) + swap(row, 2) + swap(row, 3)


def sum_row_expert(row, square):
    if not square:
        return lax.psum(row, "expert")
    total = row + cross(row, 1)
    return total + cross(total, 2) + cross(total, 4) + cross(total, 6)


def per_device(
    square,
    tokens,
    modality,
    norm_gain,
    value_proj,
    gate_proj,
    conv_taps,
    conv_bias,
    state_proj,
    step_proj,
    step_bias,
    decay_log,
    skip_gain,
    out_proj,
    cotangent,
):
    micro_count = tokens.shape[0]
    channels = value_proj.shape[2]
    micros = range(micro_count)
    values = second_hop(value_proj, first_hop(value_proj, 1, square))
    pieces = len(values)
    if square:
        place = lax.axis_index("dp")
        shard = value_proj.shape[1]
        offs = jnp.stack([(place ^ flip) * shard for flip in range(4)]).astype(jnp.int32)
    else:
        offs = jnp.zeros((1,), jnp.int32)
    kinds = modality[:, 0, ::ROWS]
    sorted_kinds = sort_kinds(kinds.reshape(-1))
    state_t = jnp.swapaxes(state_proj, 1, 2)
    conv_bias_row = conv_bias[None]
    skip_row = skip_gain[None]

    rows = tokens[:, 0].astype(F32)
    scales = lax.rsqrt(jnp.mean(rows * rows, axis=2, keepdims=True) + EPSILON)
    unit = rows * scales
    normed = (unit * norm_gain).astype(BF16)
    gathered = [lax.all_gather(normed[m], "expert", axis=0, tiled=True) for m in micros]
    upstream = [lax.all_gather(cotangent[m, 0], "expert", axis=0, tiled=True) for m in micros]
    gates_near = first_hop(gate_proj, 1, square, *values, gathered[0])
    driven_scan = []

    pre, conv, parts, proj = [], [], [], []
    for m in micros:
        pre_now, conv_now, part = value_call(
            kinds[m],
            offs,
            gathered[m],
            values,
            conv_taps,
            conv_bias_row,
            state_t,
        )
        pre.append(pre_now)
        conv.append(conv_now)
        parts.append(part)
        if m == 0:
            total = sum_chips(sum_cores(part, square), square, gathered[-1])
            proj.append(join_cores(total, square, F32))
    gates = second_hop(gate_proj, gates_near, pre[0])
    outs = second_hop(out_proj, first_hop(out_proj, 2, square, gates[-1], pre[-1]))
    gate = [gate_call(kinds[0], offs, gathered[0], gates)]
    pairs = [None] + [sum_cores(then(part, gate[0]), square) for part in parts[1:]]
    forward = []
    for m in micros:
        if m > 0:
            total = sum_chips(pairs[m], square)
            gate.append(
                gate_call(kinds[m], offs, gathered[m], gates, after=[forward[-1][1], total])
            )
            proj.append(join_cores(total, square, F32))
        forward.append(
            scan_call(
                kinds[m],
                proj[m],
                step_proj,
                step_bias,
                conv[m],
                gate[m],
                decay_log,
                skip_row,
                after=[pairs[m + 1]] if m + 1 < micro_count else (),
            )
        )
    states, scanned, step_pre, mixed_inner = zip(*forward)
    grad_out_pieces = weight_call(
        sorted_kinds, offs, upstream, mixed_inner, pieces, False, "out_weight", after=outs[-1:]
    )
    out_received = send_pieces(grad_out_pieces, 2)
    back = [
        back_out_call(
            kinds[m],
            offs,
            upstream[m],
            gate[m],
            scanned[m],
            outs,
            after=grad_out_pieces[:1] if m else (),
        )
        for m in micros
    ]
    grad_scanned, gate_back = zip(*back)
    grad_gate_pieces = weight_call(
        sorted_kinds, offs, gathered, gate_back, pieces, True, "gate_weight"
    )
    gate_received = send_pieces(grad_gate_pieces, 1)
    branch = [
        out_call(
            kinds[m], offs, mixed_inner[m], outs, after=[grad_gate_pieces[0], *out_received[:2]]
        )
        for m in micros
    ]
    branch_own = [
        lax.psum_scatter(branch[m], "expert", scatter_dimension=0, tiled=True) for m in micros
    ]

    count = kinds.shape[1]
    scan_back, projected_back, passed = [], [], []
    for m in micros:
        cuts = [(0, count)] if m < micro_count - 1 else [(count // 2, count - count // 2), (0, count // 2)]
        later = None
        for first, blocks in cuts:
            swept = scan_back_call(
                kinds[m],
                proj[m],
                step_proj,
                conv[m],
                step_pre[m],
                grad_scanned[m],
                states[m],
                decay_log,
                skip_row,
                first,
                blocks,
                later,
                after=branch + passed,
            )
            later = swept[:3]
            scan_back.append(swept[3:])
            passed = [swept[2]] + ([total] if m > 0 else [])
        if m < micro_count - 1:
            total = sum_chips(sum_cores(later[0], square), square)
            projected_back.append(join_cores(total, square, BF16))
        else:
            pair = sum_cores(later[0], square)
        driven_scan.append(later[1])
        passed += [*out_received[2:], *gate_received[:2]]
    total = sum_chips(pair, square)
    projected_back.append(join_cores(total, square, BF16))
    passed = [swept[2], pair, *gate_received[2:]]
    decay_parts, skip_parts, bias_parts, step_parts = zip(*scan_back)
    added = lambda arrays: functools.reduce(jnp.add, arrays)
    early = [
        added(step_parts).reshape(-1, channels),
        added(bias_parts),
        added(decay_parts),
        added(skip_parts),
    ]
    early_sum = sum_dp(jnp.concatenate(early, axis=0), square)

    value_back, taps_parts, conv_bias_parts, state_parts = [], [], [], []
    normed_back, normed_own = [], []
    for m in micros:
        value_now, taps_now, conv_bias_now, state_now = driven_back_call(
            kinds[m],
            projected_back[m],
            state_t,
            driven_scan[m],
            conv[m],
            pre[m],
            conv_taps,
            after=[*branch_own, normed_back[0][0]] if m else passed,
        )
        value_back.append(value_now)
        taps_parts.append(taps_now)
        conv_bias_parts.append(conv_bias_now)
        state_parts.append(state_now)
        if m == micro_count - 1:
            grad_value_pieces = weight_call(
                sorted_kinds,
                offs,
                gathered,
                value_back,
                pieces,
                True,
                "value_weight",
                halves=2 if square else 1,
            )
            late = [
                added(taps_parts),
                added(conv_bias_parts),
                added(state_parts).reshape(-1, channels),
            ]
            late_sum = sum_dp(jnp.concatenate(late, axis=0), square)
        normed_back.append(
            normed_back_call(
                kinds[m],
                offs,
                value_back[m],
                gate_back[m],
                gathered[m],
                values,
                gates,
                after=[grad_value_pieces[0], late_sum] if m else [total, early_sum],
            )
        )
        normed_own.append(
            lax.psum_scatter(normed_back[m][0], "expert", scatter_dimension=0, tiled=True)
        )
    grad_out = sum_pieces(grad_out_pieces, out_received)
    grad_gate = sum_pieces(grad_gate_pieces, gate_received)
    if square:
        grad_value = scatter_halves(grad_value_pieces)
    else:
        grad_value = sum_pieces(grad_value_pieces, send_pieces(grad_value_pieces, 1))
    gain_parts = added([one[1] for one in normed_back])
    grad_gain = sum_row_dp(sum_row_expert(gain_parts, square), square)[0] / norm_gain
    normed_own = jnp.stack(normed_own).astype(F32)

    def parted(joined, arrays):
        ends, parts = 0, []
        for array in arrays:
            parts.append(joined[ends : ends + array.shape[0]])
            ends += array.shape[0]
        return parts

    step_sum, bias_sum, decay_sum, skip_sum = parted(early_sum, early)
    taps_sum, conv_bias_sum, state_sum = parted(late_sum, late)
    scaled = normed_own * norm_gain
    upstream_own = cotangent[:, 0].astype(F32)
    grad_rows = upstream_own + scales * (
        scaled - unit * jnp.mean(scaled * unit, axis=2, keepdims=True)
    )
    mixed = rows + jnp.stack(branch_own).astype(F32)
    return (
        mixed.astype(BF16)[:, None],
        grad_rows.astype(BF16)[:, None],
        grad_gain,
        grad_value,
        grad_gate,
        taps_sum,
        conv_bias_sum[0],
        jnp.swapaxes(state_sum.reshape(state_t.shape), 1, 2),
        step_sum.reshape(step_proj.shape),
        bias_sum,
        decay_sum,
        skip_sum[0],
        grad_out,
    )


def solution(mesh):
    square = mesh.shape["dp"] == 4 and mesh.shape["expert"] == 8
    placed = (
        P(None, "dp", "expert", None),
        P(None, "dp", None),
        P(),
        P(None, "dp", "expert"),
        P(None, "dp", "expert"),
        P(None, "expert"),
        P("expert"),
        P(None, "expert", None),
        P(None, None, "expert"),
        P(None, "expert"),
        P(None, "expert"),
        P("expert"),
        P(None, "expert", "dp"),
        P(None, "dp", "expert", None),
    )
    return jax.shard_map(
        functools.partial(per_device, square),
        mesh=mesh,
        in_specs=placed,
        out_specs=(
            P(None, "dp", "expert", None),
            P(None, "dp", "expert", None),
            P(),
            P(None, "dp", "expert"),
            P(None, "dp", "expert"),
            P(None, "expert"),
            P("expert"),
            P(None, "expert", None),
            P(None, None, "expert"),
            P(None, "expert"),
            P(None, "expert"),
            P("expert"),
            P(None, "expert", "dp"),
        ),
        check_vma=False,
    )
```
